32 devices in a mesh: row: 8 (over y, x, core), col: 4 (over z).
Axes of the slice: x: 2, y: 2, z: 4, core: 2. Of those that a mesh axis runs over, the one named last changes fastest.
Arguments:
- orbitals: float32 [16384, 1024], P('row', 'col'), may hold values from -6 to 6
- point_index: int32 [8192], replicated, may hold values from 0 to 16383, as said below
- coulomb: float32 [8192, 8192], P('row', 'col'), may hold values from -0.001953125 to 0.001953125
- fitting: float32 [16384, 8192], P('row', 'col'), may hold values from -0.0625 to 0.0625
Outputs:
- exchange_out: float32 [16384, 1024], P('row', 'col')
The draws below stay inside these ranges and needn't reach their ends.
Inputs may be any that keep to these rules, and one draw needn't show every extreme that they name: `point_index`: indices are distinct. Grid index g lies in slab g // 2048. Of the 1024 consecutive points of each row panel, at most 256 lie in one slab, and in every panel exactly 256 lie in one slab.
All inputs are finite; a program needn't handle non-finite values.
Results may differ from the reference program's by a relative error of at most 0.00012.
Values sent between devices are 32-bit elements; how exact they have to be, the bound alone decides.
A program may use at most 128 MiB of HBM per device.

```python
import jax
import jax.numpy as jnp
from jax import lax

NB = 1024
P_SIZE = 8192
GS = 2048
G = 16384
PANEL = 1024
SLOT = 256
N_ROW = 8


def draw_point_index(key, part):
    key_slab = jax.random.fold_in(key, 11)
    key_shuffle = jax.random.fold_in(key, 23)
    key_rows = jax.random.fold_in(key, 37)
    slab_perms = jax.vmap(lambda k: jax.random.permutation(k, N_ROW))(jax.random.split(key_slab, N_ROW))
    position = jnp.arange(PANEL)
    which = jnp.where(position < SLOT, 0, 1 + (position - SLOT) % (N_ROW - 1))
    owners = slab_perms[:, which]
    owners = jax.vmap(lambda k, o: jax.random.permutation(k, o))(jax.random.split(key_shuffle, N_ROW), owners)
    owner_flat = owners.reshape(-1).astype(jnp.int32)
    onehot = (owner_flat[:, None] == jnp.arange(N_ROW)[None, :]).astype(jnp.int32)
    ranks = jnp.sum(jnp.where(onehot > 0, jnp.cumsum(onehot, axis=0) - 1, 0), axis=1)
    row_perms = jax.vmap(lambda k: jax.random.permutation(k, GS))(jax.random.split(key_rows, N_ROW))
    local = row_perms[owner_flat, ranks]
    return (owner_flat * GS + local).astype(jnp.int32)


def levels(own_key, extent, cuts, smallest, top_value):
    def one(dim, blocks):
        draws = jax.random.uniform(jax.random.fold_in(jax.random.fold_in(own_key, 6), dim), (blocks,), jnp.float32, smallest / len(cuts), top_value / len(cuts))
        return jnp.repeat(jnp.exp(draws), extent[dim] // blocks).reshape((-1,) + (1,) * (len(extent) - dim - 1))

    loudness = one(*cuts[0])
    for cut in cuts[1:]:
        loudness = loudness * one(*cut)
    return loudness


def scatter_about(rng, extent, spread, bound, shards=(), dtype=jnp.bfloat16):
    array = spread * jax.random.normal(rng, extent, jnp.float32)
    if shards:
        array = array * levels(rng, extent, shards, -0.22, 0.18)
    return jnp.clip(array, -bound, bound).astype(dtype)


def setup_inputs(seed: int = 0) -> dict:
    seeds = jax.random.split(jax.random.key(seed), 5)
    return {
        "orbitals": scatter_about(seeds[0], (G, NB), 1.0, 6.0, ((0, 8), (1, 4)), jnp.float32),
        "point_index": draw_point_index(jax.random.fold_in(seeds[4], 71), 0),
        "coulomb": scatter_about(seeds[2], (P_SIZE, P_SIZE), (P_SIZE * NB) ** -0.5, 0.001953125, ((0, 8), (1, 4)), jnp.float32),
        "fitting": scatter_about(seeds[3], (G, P_SIZE), P_SIZE ** -0.5, 0.0625, ((0, 8), (1, 4)), jnp.float32),
    }


def reference(orbitals, point_index, coulomb, fitting):
    picked = orbitals[point_index]
    pair = jnp.dot(picked, picked.T, precision=lax.Precision.HIGHEST, preferred_element_type=jnp.float32)
    weights = jnp.dot(coulomb * pair, picked, precision=lax.Precision.HIGHEST, preferred_element_type=jnp.float32)
    return -jnp.dot(fitting, weights, precision=lax.Precision.HIGHEST, preferred_element_type=jnp.float32)
```

```python
import jax
import jax.numpy as jnp
from jax import lax
from jax.sharding import PartitionSpec as P


def dot(a, b, contract_b):
    return lax.dot_general(
        a,
        b,
        (((1,), (contract_b,)), ((), ())),
        precision=lax.Precision.HIGH,
        preferred_element_type=jnp.float32,
    )


def split(x):
    high = lax.reduce_precision(x, 8, 7)
    return high.astype(jnp.bfloat16), (x - high).astype(jnp.bfloat16)


def plain(a, b):
    return jnp.dot(a, b, preferred_element_type=jnp.float32)


def per_device(orbitals, point_index, coulomb, fitting):
    rows = lax.axis_size("row")
    cols = lax.axis_size("col")
    ratio = rows // cols
    slab_rows, band_cols = orbitals.shape
    per_panel = point_index.shape[0] // rows
    slots = 2 * per_panel // rows
    my_row = lax.axis_index("row")
    chunks = max(1, band_cols // 128)
    width = band_cols // chunks
    perm = []
    for r in range(rows):
        for c in range(cols):
            perm.append((r * cols + c, ((r % ratio) * cols + c) * cols + r // ratio))

    owner = point_index // slab_rows
    local = (point_index - owner * slab_rows).reshape(rows, per_panel)
    owner = owner.reshape(rows, per_panel)
    mine = owner == my_row
    owner_mine = lax.dynamic_slice_in_dim(owner, my_row, 1, 0)
    held = owner_mine == jnp.arange(rows)[:, None]
    flags = jnp.concatenate([mine, held], axis=0).astype(jnp.bfloat16)
    triangle = (jnp.arange(per_panel)[:, None] <= jnp.arange(per_panel)[None, :]).astype(jnp.bfloat16)
    rank = jnp.dot(flags, triangle, preferred_element_type=jnp.float32).astype(jnp.int32) - 1
    chosen = mine[:, :, None] & (rank[:rows, :, None] == jnp.arange(slots)[None, None, :])
    source = jnp.sum(jnp.where(chosen, local[:, :, None], 0), axis=1)
    slot_mine = jnp.sum(jnp.where(held, rank[rows:], 0), axis=0)

    received = lax.all_to_all(orbitals[source], "row", split_axis=0, concat_axis=0, tiled=True)
    strip = received.reshape(rows * slots, band_cols)[owner_mine[0] * slots + slot_mine]

    def to_column(x):
        held = {0: lax.ppermute(x, ("row", "col"), perm)}
        for d in range(2, rows, 2):
            held[d] = lax.ppermute(held[0], "row", [(r, r ^ d) for r in range(rows)])
        for d in range(0, rows, 2):
            held[d + 1] = lax.ppermute(held[d], "row", [(r, r ^ 1) for r in range(rows)])
        return held

    def lay_out(held):
        w = held[0].shape[1]
        full = jnp.zeros((per_panel, rows * w), jnp.float32)
        for d in range(rows):
            full = lax.dynamic_update_slice(full, held[d], (0, (my_row ^ d) * w))
        return jnp.concatenate([full[:, j * cols * w : (j + 1) * cols * w] for j in range(ratio)], axis=0)

    panel = lax.all_gather(strip, "col", axis=1, tiled=True)
    column = lay_out(to_column(strip))
    pair = dot(panel, column, 1)
    scaled = coulomb * pair
    fitting_high, fitting_low = split(fitting)

    partial = dot(scaled, column, 0)
    outs = []
    for k in range(chunks):
        starts = [c * band_cols + k * width for c in range(cols)]
        part = jnp.concatenate([partial[:, at : at + width] for at in starts], axis=1)
        summed = lax.psum_scatter(part, "col", scatter_dimension=1, tiled=True)
        high, low = split(lay_out(to_column(summed)))
        term = plain(fitting_low, high) + plain(fitting_high, low) + plain(fitting_high, high)
        outs.append(lax.psum_scatter(-term, "col", scatter_dimension=1, tiled=True))
    return jnp.concatenate(outs, axis=1)


def solution(mesh):
    in_specs = (P("row", "col"), P(), P("row", "col"), P("row", "col"))
    return jax.shard_map(
        per_device, mesh=mesh, in_specs=in_specs, out_specs=P("row", "col"), check_vma=False
    )
```

```python
import jax
import jax.numpy as jnp
from jax import lax
from jax.sharding import PartitionSpec as P


def dot(a, b, contract_b):
    return lax.dot_general(
        a,
        b,
        (((1,), (contract_b,)), ((), ())),
        precision=lax.Precision.HIGH,
        preferred_element_type=jnp.float32,
    )


def split(x):
    high = lax.reduce_precision(x, 8, 7)
    return high.astype(jnp.bfloat16), (x - high).astype(jnp.bfloat16)


def plain(a, b):
    return jnp.dot(a, b, preferred_element_type=jnp.float32)


def per_device(orbitals, point_index, coulomb, fitting):
    rows = lax.axis_size("row")
    cols = lax.axis_size("col")
    ratio = rows // cols
    slab_rows, band_cols = orbitals.shape
    per_panel = point_index.shape[0] // rows
    slots = 2 * per_panel // rows
    my_row = lax.axis_index("row")
    chunks = max(1, band_cols // 128)
    width = band_cols // chunks
    wide = width * cols
    perm = []
    for r in range(rows):
        for c in range(cols):
            perm.append((r * cols + c, ((r % ratio) * cols + c) * cols + r // ratio))

    owner = point_index // slab_rows
    local = (point_index - owner * slab_rows).reshape(rows, per_panel)
    owner = owner.reshape(rows, per_panel)
    mine = owner == my_row
    owner_mine = lax.dynamic_slice_in_dim(owner, my_row, 1, 0)
    held = owner_mine == jnp.arange(rows)[:, None]
    flags = jnp.concatenate([mine, held], axis=0).astype(jnp.bfloat16)
    triangle = (jnp.arange(per_panel)[:, None] <= jnp.arange(per_panel)[None, :]).astype(jnp.bfloat16)
    rank = jnp.dot(flags, triangle, preferred_element_type=jnp.float32).astype(jnp.int32) - 1
    chosen = mine[:, :, None] & (rank[:rows, :, None] == jnp.arange(slots)[None, None, :])
    source = jnp.sum(jnp.where(chosen, local[:, :, None], 0), axis=1)
    slot_mine = jnp.sum(jnp.where(held, rank[rows:], 0), axis=0)

    received = lax.all_to_all(orbitals[source], "row", split_axis=0, concat_axis=0, tiled=True)
    strip = received.reshape(rows * slots, band_cols)[owner_mine[0] * slots + slot_mine]

    def to_column(x):
        held = {0: lax.ppermute(x, ("row", "col"), perm)}
        for d in range(2, rows, 2):
            held[d] = lax.ppermute(held[0], "row", [(r, r ^ d) for r in range(rows)])
        for d in range(0, rows, 2):
            held[d + 1] = lax.ppermute(held[d], "row", [(r, r ^ 1) for r in range(rows)])
        return held

    def lay_out(held, start):
        full = jnp.zeros((per_panel, rows * width), jnp.float32)
        for d in range(rows):
            part = held[d][:, start : start + width]
            full = lax.dynamic_update_slice(full, part, (0, (my_row ^ d) * width))
        return jnp.concatenate([full[:, j * wide : (j + 1) * wide] for j in range(ratio)], axis=0)

    arrived = to_column(strip)
    column = [lay_out(arrived, k * width) for k in range(chunks)]
    panel = lax.all_gather(strip, "col", axis=1, tiled=True)
    panel = panel.reshape(per_panel, cols, chunks, width)
    pair = 0
    for k in range(chunks):
        pair = pair + dot(panel[:, :, k].reshape(per_panel, wide), column[k], 1)
    scaled = coulomb * pair
    fitting_high, fitting_low = split(fitting)

    outs = []
    for k in range(chunks):
        partial = dot(scaled, column[k], 0)
        summed = lax.psum_scatter(partial, "col", scatter_dimension=1, tiled=True)
        high, low = split(lay_out(to_column(summed), 0))
        term = plain(fitting_low, high) + plain(fitting_high, low) + plain(fitting_high, high)
        outs.append(lax.psum_scatter(-term, "col", scatter_dimension=1, tiled=True))
    return jnp.concatenate(outs, axis=1)


def solution(mesh):
    in_specs = (P("row", "col"), P(), P("row", "col"), P("row", "col"))
    return jax.shard_map(
        per_device, mesh=mesh, in_specs=in_specs, out_specs=P("row", "col"), check_vma=False
    )
```
